128 devices in a mesh: pair: 8 (over y_hi, x), virt: 8 (over y_lo, z), rep: 2 (over core).
Axes of the slice: x: 4, y: 4 (y_hi: 2, y_lo: 2; y = y_hi * 2 + y_lo), z: 4, core: 2. Of those that a mesh axis runs over, the one named last changes fastest.
Arguments:
- amplitudes: bfloat16 [8, 8, 1024, 1024], P('pair', None, None, 'virt'), may hold values from -6 to 6
- tile_mask: int32 [8, 8, 8, 8], replicated, may hold values from 0 to 1, as said below
- hole_integrals: bfloat16 [8, 1024, 8, 1024], P('pair', None, None, 'virt'), may hold values from -0.0625 to 0.0625
- virt_fock: bfloat16 [1024, 1024], P('virt'), may hold values from -0.1875 to 0.1875
- occ_energy: float32 [8], replicated, may hold values from -4 to -0.5
- virt_energy: float32 [1024], replicated, may hold values from 0.5 to 4
Outputs:
- new_amplitudes: float32 [8, 8, 1024, 1024], P('pair', None, 'rep', 'virt')
The draws below stay inside these ranges and needn't reach their ends.
Inputs may be any that keep to these rules, and one draw needn't show every extreme that they name: `tile_mask`: entries are 0 or 1; tiles whose two virtual tile indices are equal are always 1; the share of kept tiles differs from one first occupied index to another.
All inputs are finite; a program needn't handle non-finite values.
Results may differ from the reference program's by a relative error of at most 0.0013.
Values may be sent and summed in bfloat16 or wider, within the bound.
No kernel may reach another device: no remote copies, remote signals or barrier semaphores. Data moves between devices by JAX's collectives and lax.ppermute only.
A program may use at most 128 MiB of HBM per device.

```python
import math
import jax
import jax.numpy as jnp
from jax import lax

V = 1024
TILE = 128
OCC = 8
NVT = 8


def draw_tile_mask(key, part):
    key = jax.random.fold_in(key, 11)
    first_key, second_key = jax.random.split(key)
    shares = jax.random.randint(first_key, (OCC, 1, 1, 1), 20, 95)
    rolls = jax.random.randint(second_key, (OCC, OCC, NVT, NVT), 0, 100)
    across = jnp.arange(NVT)[:, None] == jnp.arange(NVT)[None, :]
    kept = (rolls < shares) | across[None, None, :, :]
    return kept.astype(jnp.int32)


def steps_of(rng, extent, shards, smallest, top_value):
    factor_of = 1.0
    for dim, parts in shards:
        steps = jax.random.uniform(jax.random.fold_in(jax.random.fold_in(rng, 6), dim), (parts,), jnp.float32, smallest / len(shards), top_value / len(shards))
        factor_of = factor_of * jnp.repeat(jnp.exp(steps), extent[dim] // parts).reshape((-1,) + (1,) * (len(extent) - 1 - dim))
    return factor_of


def centred(stream_key, dims, deviation, bound, shards=(), held_as=jnp.bfloat16):
    result = deviation * jax.random.normal(stream_key, dims, jnp.float32)
    if shards:
        result = result * steps_of(stream_key, dims, shards, -0.22, 0.18)
    return jnp.clip(result, -bound, bound).astype(held_as)


def setup_inputs(seed: int = 0) -> dict:
    key_list = jax.random.split(jax.random.key(seed), 7)
    return {
        "amplitudes": centred(key_list[0], (OCC, OCC, V, V), 1.0, 6.0, ((0, 8), (3, 8))),
        "tile_mask": draw_tile_mask(jax.random.fold_in(key_list[6], 71), 0),
        "hole_integrals": centred(key_list[2], (OCC, V, OCC, V), (OCC * V) ** -0.5, 0.0625, ((0, 8), (3, 8))),
        "virt_fock": centred(key_list[3], (V, V), V ** -0.5, 0.1875, ((0, 8),)),
        "occ_energy": jnp.clip(jax.random.uniform(key_list[4], (OCC,), jnp.float32, -4.0, -0.5), -4.0, -0.5),
        "virt_energy": jnp.clip(jnp.exp(jax.random.uniform(key_list[5], (V,), jnp.float32, math.log(0.5), math.log(4.0))), 0.5, 4.0),
    }


def expand_tiles(flags, tile_width):
    lead_dim, second_dim, across_dim, down_dim = flags.shape
    spread = jnp.broadcast_to(flags[:, :, :, None, :, None], (lead_dim, second_dim, across_dim, tile_width, down_dim, tile_width))
    return spread.reshape(lead_dim, second_dim, across_dim * tile_width, down_dim * tile_width)


def reference(amplitudes, tile_mask, hole_integrals, virt_fock, occ_energy, virt_energy):
    keep = expand_tiles(tile_mask.astype(jnp.bfloat16), TILE)
    masked = amplitudes * keep
    flat_integrals = hole_integrals.reshape(OCC * V, OCC * V)
    fock_right = virt_fock.T

    def one_row(row_index):
        slab_amps = masked[row_index]
        left_side = jnp.transpose(slab_amps, (1, 0, 2)).reshape(V, OCC * V)
        hole_term = jnp.dot(left_side, flat_integrals, preferred_element_type=jnp.float32)
        hole_term = jnp.transpose(hole_term.reshape(V, OCC, V), (1, 0, 2))
        fock_term = jnp.dot(slab_amps.reshape(OCC * V, V), fock_right, preferred_element_type=jnp.float32).reshape(OCC, V, V)
        residual = keep[row_index].astype(jnp.float32) * (hole_term + fock_term)
        denominator = virt_energy[None, :, None] + virt_energy[None, None, :] - occ_energy[row_index] - occ_energy[:, None, None]
        return slab_amps.astype(jnp.float32) + residual / denominator

    return lax.map(one_row, jnp.arange(OCC).astype(jnp.int32))
```

```python
import functools

import jax
import jax.numpy as jnp
from jax import lax
from jax.experimental import pallas as pl
from jax.experimental.pallas import tpu as pltpu
from jax.sharding import PartitionSpec as P

TILE = 128
AXES = ("pair", "virt", "rep")
X = Z = 4


def device_permutation(move):
    pairs = []
    for index in range(128):
        p, v, core = index // 16, (index // 2) % 8, index % 2
        y, x, z, core = move((p // 4) * 2 + v // 4, p % 4, v % 4, core)
        pairs.append((index, ((y // 2) * 4 + x % 4) * 16 + ((y % 2) * 4 + z % 4) * 2 + core))
    return pairs


def step_of(core):
    return 1 if core == 0 else -1


ALONG_X = device_permutation(lambda y, x, z, c: (y, x + step_of(c), z, c))
ALONG_Z = device_permutation(lambda y, x, z, c: (y, x, z + step_of(c), c))
Y_LOW = device_permutation(lambda y, x, z, c: (y ^ 1, x, z, c))
Y_HIGH = device_permutation(lambda y, x, z, c: (y ^ 2, x, z, c))
CORES = device_permutation(lambda y, x, z, c: (y, x, z, 1 - c))


def send(block, permutation):
    return lax.ppermute(block, AXES, permutation)


def partial_kernel(where, *refs):
    left, right = refs[0:8], refs[8:16]
    fock_ref, out_ref, a_all, b_all, sems = refs[16:]
    rows = out_ref.shape[1]
    core, row_start = where[0], pl.multiple_of(where[1], rows)
    copies = []
    for slot in range(8):
        copies.append(
            pltpu.make_async_copy(right[slot], b_all.at[where[10 + slot]], sems.at[slot])
        )
        copies.append(
            pltpu.make_async_copy(
                left[slot].at[:, pl.ds(row_start, rows), :],
                a_all.at[where[2 + slot]],
                sems.at[8 + slot],
            )
        )
    for copy in copies:
        copy.start()
    for copy in copies:
        copy.wait()
    block = 256

    def tile(step, carry):
        pair_j, row_block = step // (rows // block), step % (rows // block)
        row = pl.multiple_of(row_block * block, block)
        total = jnp.zeros((block, 2 * TILE), jnp.float32)
        for v in range(8):
            odd = (core + v) % 2
            lhs = jnp.concatenate([a_all[v, m, pl.ds(row, block), :] for m in range(4)], axis=1)
            rhs = jnp.concatenate(
                [
                    jnp.concatenate(
                        [b_all[2 * m + odd, v // 2, 2 * pair_j + h] for h in range(2)], axis=1
                    )
                    for m in range(4)
                ],
                axis=0,
            )
            total += jnp.dot(lhs, rhs, preferred_element_type=jnp.float32)
        for h in range(2):
            first = (core + h) % 2
            lhs = jnp.concatenate(
                [a_all[2 * t + first, pair_j, pl.ds(row, block), :] for t in range(4)], axis=1
            )
            rhs = jnp.concatenate(
                [
                    fock_ref[pl.ds(pl.multiple_of((2 * t + first) * TILE, TILE), TILE), :]
                    for t in range(4)
                ],
                axis=0,
            )
            fock = jnp.dot(lhs, rhs, preferred_element_type=jnp.float32)
            out_ref[2 * pair_j + h, pl.ds(row, block), :] = (
                total[:, h * TILE : (h + 1) * TILE] + fock
            )
        return carry

    lax.fori_loop(0, 4 * (rows // block), tile, 0)


def partial_sums(where, left, right, fock_columns, rows):
    anywhere = pl.BlockSpec(memory_space=pl.ANY)
    return pl.pallas_call(
        partial_kernel,
        out_shape=jax.ShapeDtypeStruct((8, rows, TILE), jnp.float32),
        in_specs=[pl.BlockSpec(memory_space=pltpu.SMEM)]
        + [anywhere] * 16
        + [pl.BlockSpec(memory_space=pltpu.VMEM)],
        out_specs=pl.BlockSpec(memory_space=pltpu.VMEM),
        scratch_shapes=[
            pltpu.VMEM((8, 4, rows, TILE), jnp.bfloat16),
            pltpu.VMEM((8, 4, 8, TILE, TILE), jnp.bfloat16),
            pltpu.SemaphoreType.DMA((16,)),
        ],
        compiler_params=pltpu.CompilerParams(vmem_limit_bytes=48 * 2**20),
        cost_estimate=pl.CostEstimate(
            flops=2 * rows * 1024 * 4608, bytes_accessed=24 * 2**20, transcendentals=0
        ),
        name="partial_sums",
    )(where, *left, *right, fock_columns)


def local(amplitudes, tile_mask, hole_integrals, virt_fock, occ_energy, virt_energy):
    p, v, r = (lax.axis_index(name) for name in AXES)
    rows = 512
    flags = lax.dynamic_slice(tile_mask, (p, 0, 0, v), (1, 8, 8, 1)).reshape(8, 8)
    odd = (r + v) % 2
    own_flags = lax.dynamic_index_in_dim(flags.reshape(4, 2, 8), odd, 1, keepdims=False)
    own_amps = lax.dynamic_index_in_dim(
        amplitudes.reshape(4, 2, 1024, TILE), odd, 1, keepdims=False
    )
    keep_rows = jnp.broadcast_to(own_flags[:, :, None], (4, 8, TILE)).reshape(4, 1024, 1)
    left_own = own_amps * keep_rows.astype(jnp.bfloat16)
    right_own = lax.dynamic_index_in_dim(
        hole_integrals.reshape(4, 2, TILE, 8, TILE), (r + p) % 2, 1, keepdims=False
    ).transpose(0, 2, 1, 3)

    left_far, right_far = send(left_own, Y_LOW), send(right_own, Y_HIGH)
    left, right = [left_own], [right_own]
    left_p, right_p = [left_far], [right_far]
    for _ in range(3):
        left.append(send(left[-1], ALONG_Z))
        right.append(send(right[-1], ALONG_X))
        left_p.append(send(left_p[-1], ALONG_Z))
        right_p.append(send(right_p[-1], ALONG_X))

    step = 1 - 2 * r
    near_z = [(v // 4) * 4 + (v - q * step) % 4 for q in range(4)]
    near_x = [(p // 4) * 4 + (p - q * step) % 4 for q in range(4)]
    places = near_z + [(t + 4) % 8 for t in near_z] + near_x + [(t + 4) % 8 for t in near_x]
    fock_columns = virt_fock.T

    def half(which):
        where = jnp.stack([r, which * rows] + places).astype(jnp.int32)
        return partial_sums(where, left + left_p, right + right_p, fock_columns, rows)

    other_part = half(1 - r)
    arrived = send(other_part, CORES)
    total = half(r) + arrived

    row_start = r * rows
    keep_half = jnp.broadcast_to(
        lax.dynamic_slice_in_dim(flags, r * 4, 4, 1)[:, :, None], (8, 4, TILE)
    ).reshape(1, 8, rows, 1)
    amps_half = lax.dynamic_slice_in_dim(amplitudes, row_start, rows, 2)
    masked_half = amps_half * keep_half.astype(jnp.bfloat16)
    residual = keep_half.astype(jnp.float32) * total[None]
    occ_own = lax.dynamic_slice_in_dim(occ_energy, p, 1, 0)
    virt_rows = lax.dynamic_slice_in_dim(virt_energy, row_start, rows, 0)
    virt_cols = lax.dynamic_slice_in_dim(virt_energy, v * TILE, TILE, 0)
    denominator = (
        virt_rows[None, None, :, None]
        + virt_cols[None, None, None, :]
        - occ_own[:, None, None, None]
        - occ_energy[None, :, None, None]
    )
    return masked_half.astype(jnp.float32) + residual / denominator


def solution(mesh):
    return jax.shard_map(
        local,
        mesh=mesh,
        in_specs=(
            P("pair", None, None, "virt"),
            P(),
            P("pair", None, None, "virt"),
            P("virt", None),
            P(),
            P(),
        ),
        out_specs=P("pair", None, "rep", "virt"),
        check_vma=False,
    )
```

```python
import functools

import jax
import jax.numpy as jnp
from jax import lax
from jax.experimental import pallas as pl
from jax.experimental.pallas import tpu as pltpu
from jax.sharding import PartitionSpec as P

TILE = 128
AXES = ("pair", "virt", "rep")


def device_permutation(move):
    pairs = []
    for index in range(128):
        p, v, core = index // 16, (index // 2) % 8, index % 2
        y, x, z, core = move((p // 4) * 2 + v // 4, p % 4, v % 4, core)
        pairs.append((index, ((y // 2) * 4 + x % 4) * 16 + ((y % 2) * 4 + z % 4) * 2 + core))
    return pairs


def step_of(core):
    return 1 if core == 0 else -1


ALONG_X = device_permutation(lambda y, x, z, c: (y, x + step_of(c), z, c))
ALONG_Z = device_permutation(lambda y, x, z, c: (y, x, z + step_of(c), c))
Y_LOW = device_permutation(lambda y, x, z, c: (y ^ 1, x, z, c))
Y_HIGH = device_permutation(lambda y, x, z, c: (y ^ 2, x, z, c))
CORES = device_permutation(lambda y, x, z, c: (y, x, z, 1 - c))


def send(block, permutation):
    return lax.ppermute(block, AXES, permutation)


def gate_kernel(*refs):
    pass


def gate(passed, after):
    anywhere = pl.BlockSpec(memory_space=pl.ANY)
    return pl.pallas_call(
        gate_kernel,
        out_shape=[jax.ShapeDtypeStruct(x.shape, x.dtype) for x in passed],
        in_specs=[anywhere] * (len(passed) + len(after)),
        out_specs=[anywhere] * len(passed),
        input_output_aliases={i: i for i in range(len(passed))},
        name="gate",
    )(*passed, *after)


def assemble(where, left, right, near, full, a_all, b_all, sems):
    p, v, core = where[0], where[1], where[2]
    step = 1 - 2 * core
    low = v // 4 if near[0] else 1 - v // 4
    high = p // 4 if near[1] else 1 - p // 4
    left_start = 2 * high if full[0] else 0
    right_start = pl.multiple_of(256 * low, 256) if full[1] else 0
    copies = []
    for q in range(4):
        x = (p + 4 - q * step) % 4
        copies.append(
            pltpu.make_async_copy(
                right[q].at[pl.ds(right_start, 256), :],
                b_all.at[pl.ds(pl.multiple_of(x * 256, 256), 256), :],
                sems.at[q],
            )
        )
        z = (v + 4 - q * step) % 4
        for m in range(2):
            x = 2 * m + (core + z) % 2
            copies.append(
                pltpu.make_async_copy(
                    left[q].at[left_start + m],
                    a_all.at[:, pl.ds(pl.multiple_of((2 * x + z // 2) * TILE, TILE), TILE)],
                    sems.at[4 + 2 * q + m],
                )
            )
    for copy in copies:
        copy.start()
    for copy in copies:
        copy.wait()


def multiply(where, near, fock_ref, acc_ref, out_ref, a_all, b_all, row_start):
    p, v, core = where[0], where[1], where[2]
    low = v // 4 if near[0] else 1 - v // 4
    high = p // 4 if near[1] else 1 - p // 4
    rows, width, block = out_ref.shape[0], 256, 512

    def columns_of(step, carry):
        columns = pl.ds(pl.multiple_of(step * width, width), width)
        for row in range(0, rows, block):
            part = pl.ds(row, block)
            source = pl.ds(row_start + row, block)
            total = jnp.dot(a_all[source, :], b_all[:, columns], preferred_element_type=jnp.float32)
            if acc_ref is not None:
                total += acc_ref[source, columns]
            out_ref[part, columns] = total
        return carry

    lax.fori_loop(0, 1024 // width, columns_of, 0)
    for x in range(4):
        fock = jnp.concatenate(
            [
                fock_ref[
                    pl.ds(pl.multiple_of((4 * low + 2 * t + (x + core) % 2) * TILE, TILE), TILE), :
                ]
                for t in range(2)
            ],
            axis=0,
        )
        columns = pl.ds(pl.multiple_of((4 * high + x) * TILE, TILE), TILE)
        for row in range(0, rows, block):
            out_ref[pl.ds(row, block), columns] += jnp.dot(
                a_all[pl.ds(row_start + row, block), x * 256 : (x + 1) * 256],
                fock,
                preferred_element_type=jnp.float32,
            )


def quarter_kernel(start_from, near, full, where, *refs):
    left, right, fock_ref = refs[0:4], refs[4:8], refs[8]
    refs = refs[9:]
    acc_ref = None
    if start_from:
        acc_ref, refs = refs[0], refs[1:]
    out_ref, a_all, b_all, sems = refs
    assemble(where, left, right, near, full, a_all, b_all, sems)
    multiply(where, near, fock_ref, acc_ref, out_ref, a_all, b_all, 0)


def last_kernel(near, full, where, *refs):
    left, right = refs[0:4], refs[4:8]
    fock_ref, acc_ref, out_ref, a_all, b_all, sems = refs[8:]
    assemble(where, left, right, near, full, a_all, b_all, sems)
    row_start = pl.multiple_of((1 - where[2]) * 512, 512)
    multiply(where, near, fock_ref, acc_ref, out_ref, a_all, b_all, row_start)


def rest_kernel(near, where, a_all, b_all, fock_ref, acc_ref, out_ref):
    row_start = pl.multiple_of(where[2] * 512, 512)
    multiply(where, near, fock_ref, acc_ref, out_ref, a_all, b_all, row_start)


ANYWHERE = pl.BlockSpec(memory_space=pl.ANY)
VMEM = pl.BlockSpec(memory_space=pltpu.VMEM)
SMEM = pl.BlockSpec(memory_space=pltpu.SMEM)
LIMIT = pltpu.CompilerParams(vmem_limit_bytes=32 * 2**20)


def cost(rows):
    return pl.CostEstimate(
        flops=2 * rows * 1024 * 1280, bytes_accessed=8 * 2**20, transcendentals=0
    )


def add_quarter(acc, where, left, right, fock_columns, near, full):
    start_from = acc is not None
    return pl.pallas_call(
        functools.partial(quarter_kernel, start_from, near, full),
        in_specs=[SMEM] + [ANYWHERE] * 8 + [VMEM] * (1 + start_from),
        out_specs=VMEM,
        scratch_shapes=[
            pltpu.VMEM((1024, 1024), jnp.bfloat16),
            pltpu.VMEM((1024, 1024), jnp.bfloat16),
            pltpu.SemaphoreType.DMA((12,)),
        ],
        out_shape=jax.ShapeDtypeStruct((1024, 1024), jnp.float32),
        input_output_aliases={10: 0} if start_from else {},
        compiler_params=LIMIT,
        cost_estimate=cost(1024),
        name="add_quarter",
    )(where, *left, *right, fock_columns, *([acc] * start_from))


def last_quarter(acc, where, left, right, fock_columns, near, full):
    return pl.pallas_call(
        functools.partial(last_kernel, near, full),
        in_specs=[SMEM] + [ANYWHERE] * 8 + [VMEM] * 2,
        out_specs=[VMEM] * 3,
        scratch_shapes=[pltpu.SemaphoreType.DMA((12,))],
        out_shape=[
            jax.ShapeDtypeStruct((512, 1024), jnp.float32),
            jax.ShapeDtypeStruct((1024, 1024), jnp.bfloat16),
            jax.ShapeDtypeStruct((1024, 1024), jnp.bfloat16),
        ],
        compiler_params=LIMIT,
        cost_estimate=cost(512),
        name="last_quarter",
    )(where, *left, *right, fock_columns, acc)


def rest_of_quarter(acc, where, a_all, b_all, fock_columns, near):
    return pl.pallas_call(
        functools.partial(rest_kernel, near),
        in_specs=[SMEM] + [VMEM] * 4,
        out_specs=VMEM,
        out_shape=jax.ShapeDtypeStruct((512, 1024), jnp.float32),
        compiler_params=LIMIT,
        cost_estimate=cost(512),
        name="rest_of_quarter",
    )(where, a_all, b_all, fock_columns, acc)


def update_kernel(where, flags_ref, occ_ref, virt_ref, own_ref, other_ref, amps_ref, out_ref, amps, new, sems):
    p, v, core = where[0], where[1], where[2]
    row_start = pl.multiple_of(core * 512, 512)
    load = pltpu.make_async_copy(amps_ref.at[0, :, pl.ds(row_start, 512), :], amps, sems.at[8])
    load.start()
    across = jnp.transpose(virt_ref[...])
    rows = [jnp.where(core == 0, across[:, t : t + 1], across[:, t + 4 : t + 5]) for t in range(4)]
    base = virt_ref[pl.ds(v, 1), :] - occ_ref[p]
    sums = [jnp.broadcast_to(row, (TILE, TILE)) + base for row in rows]
    load.wait()
    stores = []
    for j in range(8):
        for t in range(4):
            part = slice(t * TILE, (t + 1) * TILE)
            columns = slice(j * TILE, (j + 1) * TILE)
            keep = flags_ref[j, 4 * core + t].astype(jnp.float32)
            masked = amps[j, part, :].astype(jnp.float32) * keep
            residual = keep * (own_ref[part, columns] + other_ref[part, columns])
            new[j, part, :] = masked + residual / (sums[t] - occ_ref[j])
        store = pltpu.make_async_copy(new.at[j], out_ref.at[0, j], sems.at[j])
        store.start()
        stores.append(store)
    for store in stores:
        store.wait()


def update(where, flags, occ_energy, virt_energy, own_part, arrived, amplitudes):
    return pl.pallas_call(
        update_kernel,
        in_specs=[SMEM, SMEM, SMEM, VMEM, VMEM, VMEM, ANYWHERE],
        out_specs=ANYWHERE,
        out_shape=jax.ShapeDtypeStruct((1, 8, 512, TILE), jnp.float32),
        scratch_shapes=[
            pltpu.VMEM((8, 512, TILE), jnp.bfloat16),
            pltpu.VMEM((8, 512, TILE), jnp.float32),
            pltpu.SemaphoreType.DMA((9,)),
        ],
        compiler_params=LIMIT,
        name="update",
    )(where, flags, occ_energy, virt_energy, own_part, arrived, amplitudes)


def local(amplitudes, tile_mask, hole_integrals, virt_fock, occ_energy, virt_energy):
    p, v, r = (lax.axis_index(name) for name in AXES)
    rows = 512
    flags = lax.dynamic_slice(tile_mask, (p, 0, 0, v), (1, 8, 8, 1)).reshape(8, 8)
    odd = (r + v) % 2
    own_flags = lax.dynamic_index_in_dim(flags.reshape(4, 2, 8), odd, 1, keepdims=False)
    own_amps = lax.dynamic_index_in_dim(
        amplitudes.reshape(4, 2, 1024, TILE), odd, 1, keepdims=False
    )
    keep_rows = jnp.broadcast_to(own_flags[:, :, None], (4, 8, TILE)).reshape(4, 1024, 1)
    left_own = own_amps * keep_rows.astype(jnp.bfloat16)
    right_own = lax.dynamic_index_in_dim(
        hole_integrals.reshape(4, 2, TILE, 8, TILE), (r + p) % 2, 1, keepdims=False
    ).reshape(512, 1024)

    low, high = v // 4, p // 4

    def part_of(block, start, size):
        return lax.dynamic_slice_in_dim(block, start, size, 0)

    where = jnp.stack([p, v, r]).astype(jnp.int32)
    fock_columns = virt_fock.T

    left, right = [left_own], [right_own]
    right_a = [send(part_of(right_own, 256 * low, 256), Y_HIGH)]
    right.append(send(right[-1], ALONG_X))
    left.append(send(left[-1], ALONG_Z))
    right_a[0], left_a = gate([right_a[0], part_of(left_own, 2 * high, 2)], [left[1], right[1]])
    left_a = [send(left_a, Y_LOW)]
    for _ in range(2):
        right.append(send(right[-1], ALONG_X))
        left.append(send(left[-1], ALONG_Z))
    left_a[0], left_b = gate([left_a[0], part_of(left_own, 2 - 2 * high, 2)], [])
    left_b = [send(left_b, Y_LOW)]
    left_b[0], right_b = gate(
        [left_b[0], part_of(right_own, 256 - 256 * low, 256)], [left[2], right[2]]
    )
    right_b = [send(right_b, Y_HIGH)]
    for _ in range(3):
        for block in (left_a, left_b):
            block.append(send(block[-1], ALONG_Z))
        for block in (right_a, right_b):
            block.append(send(block[-1], ALONG_X))

    acc = add_quarter(None, where, left, right, fock_columns, (1, 1), (1, 1))
    acc = add_quarter(acc, where, left, right_a, fock_columns, (1, 0), (1, 0))
    acc = add_quarter(acc, where, left_a, right, fock_columns, (0, 1), (0, 1))
    far, small = (0, 0), (0, 0)
    other_part, a_all, b_all = last_quarter(acc, where, left_b, right_b, fock_columns, far, small)
    arrived = send(other_part, CORES)
    own_part = rest_of_quarter(acc, where, a_all, b_all, fock_columns, far)
    return update(where, flags, occ_energy, virt_energy.reshape(8, TILE), own_part, arrived, amplitudes)


def solution(mesh):
    return jax.shard_map(
        local,
        mesh=mesh,
        in_specs=(
            P("pair", None, None, "virt"),
            P(),
            P("pair", None, None, "virt"),
            P("virt", None),
            P(),
            P(),
        ),
        out_specs=P("pair", None, "rep", "virt"),
        check_vma=False,
    )
```

```python
import functools

import jax
import jax.numpy as jnp
from jax import lax
from jax.experimental import pallas as pl
from jax.experimental.pallas import tpu as pltpu
from jax.sharding import PartitionSpec as P

TILE = 128
GATE, STAY = 7, 6
AXES = ("pair", "virt", "rep")


def device_permutation(move):
    pairs = []
    for index in range(128):
        p, v, core = index // 16, (index // 2) % 8, index % 2
        y, x, z, core = move((p // 4) * 2 + v // 4, p % 4, v % 4, core)
        pairs.append((index, ((y // 2) * 4 + x % 4) * 16 + ((y % 2) * 4 + z % 4) * 2 + core))
    return pairs


def ring_next(plane, place, cross):
    if plane == 0:
        return (1, place) if place == cross else (0, (place + 1) % 4)
    return (0, place) if place == (cross + 1) % 4 else (1, (place + 3) % 4)


def ring_move(plane, place, cross, core):
    if core == 0:
        return ring_next(plane, place, cross)
    return next(
        (a, b) for a in range(2) for b in range(4) if ring_next(a, b, cross) == (plane, place)
    )


def along_virt(y, x, z, core):
    low, z = ring_move(y % 2, z, 0 if x < 2 else 2, core)
    return (y // 2) * 2 + low, x, z, core


def along_pair(y, x, z, core):
    high, x = ring_move(y // 2, x, 2 if z < 2 else 0, core)
    return high * 2 + y % 2, x, z, core


ALONG_VIRT = device_permutation(along_virt)
ALONG_PAIR = device_permutation(along_pair)
CORES = device_permutation(lambda y, x, z, c: (y, x, z, 1 - c))


def send(block, permutation):
    return lax.ppermute(block, AXES, permutation)


def bit_of(index):
    return (index + index // 4) % 2


def on_ring(index, cross, core, step):
    plane, place = index // 4, index % 4
    spot = jnp.where(plane == 0, (place - cross + 3) % 4, 4 + (cross - place + 4) % 4)
    spot = (spot + 8 - (1 - 2 * core) * step) % 8
    return jnp.where(spot < 4, (spot + cross + 1) % 4, 4 + (cross - spot + 8) % 4)


class Tiles:
    def __init__(self, where, items):
        p, v, core = where[0], where[1], where[2]
        self.items = items
        self.odd = (core + bit_of(p) + bit_of(v)) % 2
        cross = jnp.where(p % 4 < 2, 0, 2)
        self.v = [on_ring(v, cross, core, q) for q in range(8)]
        cross = jnp.where(v % 4 < 2, 2, 0)
        self.k = [on_ring(p, cross, core, q) for q in range(8)]

    def pairs(self, item):
        i, j = self.items[item]
        for t in range(2):
            second = (self.odd + t) % 2
            k = jnp.where(second == 0, self.k[2 * j], self.k[2 * j + 1])
            yield t, 2 * i + t, self.v[2 * i + t], second, k


def start_left(tiles, left, a_all, sems, row_start, rows):
    part = pl.ds(row_start, rows)
    for item in range(len(tiles.items)):
        for t, q, _, _, k in tiles.pairs(item):
            for half in range(2):

                @pl.when(k // 4 == half)
                def _():
                    pltpu.make_async_copy(
                        left[q][half].at[(k % 4) // 2, part, :],
                        a_all.at[part, (2 * item + t) * TILE : (2 * item + t + 1) * TILE],
                        sems.at[item, t],
                    ).start()

    def wait(item):
        i = tiles.items[item][0]
        for t in range(2):
            pltpu.make_async_copy(
                left[2 * i + t][0].at[0, part, :],
                a_all.at[part, (2 * item + t) * TILE : (2 * item + t + 1) * TILE],
                sems.at[item, t],
            ).wait()

    return wait


def start_right(tiles, right, b_all, sems):
    for item in range(len(tiles.items)):
        j = tiles.items[item][1]
        for t, _, v, second, _ in tiles.pairs(item):
            for which in range(2):
                for half in range(2):

                    @pl.when((second == which) & (v // 4 == half))
                    def _():
                        rows = pl.ds(pl.multiple_of(((v % 4) // 2) * TILE, TILE), TILE)
                        pltpu.make_async_copy(
                            right[2 * j + which][half].at[rows, :],
                            b_all.at[(2 * item + t) * TILE : (2 * item + t + 1) * TILE, :],
                            sems.at[item, t],
                        ).start()

    def wait(item):
        j = tiles.items[item][1]
        for t in range(2):
            pltpu.make_async_copy(
                right[2 * j][0].at[pl.ds(0, TILE), :],
                b_all.at[(2 * item + t) * TILE : (2 * item + t + 1) * TILE, :],
                sems.at[item, t],
            ).wait()

    return wait


def multiply(tiles, fock_ref, acc_ref, out_ref, a_all, b_all, row_start):
    rows, width, block = out_ref.shape[0], 256, 512

    def columns_of(step, carry):
        columns = pl.ds(pl.multiple_of(step * width, width), width)
        for row in range(0, rows, block):
            source = pl.ds(row_start + row, block)
            total = jnp.dot(a_all[source, :], b_all[:, columns], preferred_element_type=jnp.float32)
            if acc_ref is not None:
                total += acc_ref[source, columns]
            out_ref[pl.ds(row, block), columns] = total
        return carry

    lax.fori_loop(0, 1024 // width, columns_of, 0)
    blank = jnp.zeros((TILE, TILE), jnp.bfloat16)
    for item in range(len(tiles.items)):
        fock, places = [], []
        for t, _, v, _, k in tiles.pairs(item):
            own = fock_ref[pl.ds(pl.multiple_of(v * TILE, TILE), TILE), :]
            fock.append(jnp.concatenate([own, blank] if t == 0 else [blank, own], axis=1))
            places.append(pl.ds(pl.multiple_of(k * TILE, TILE), TILE))
        fock = jnp.concatenate(fock, axis=0)
        for row in range(0, rows, block):
            part = pl.ds(row, block)
            left = a_all[pl.ds(row_start + row, block), item * 256 : (item + 1) * 256]
            total = jnp.dot(left, fock, preferred_element_type=jnp.float32)
            for t in range(2):
                out_ref[part, places[t]] += total[:, t * TILE : (t + 1) * TILE]


def gate_kernel(*refs):
    pass


def gate(passed, after):
    return pl.pallas_call(
        gate_kernel,
        out_shape=[jax.ShapeDtypeStruct(x.shape, x.dtype) for x in passed],
        in_specs=[ANYWHERE] * (len(passed) + len(after)),
        out_specs=[ANYWHERE] * len(passed),
        input_output_aliases={i: i for i in range(len(passed))},
        name="gate",
    )(*passed, *after)


def paired(refs):
    return [refs[n : n + 2] for n in range(0, len(refs), 2)]


def part_kernel(start_from, items, count, where, *refs):
    left, right = paired(refs[: 2 * count]), paired(refs[2 * count : 4 * count])
    fock_ref, refs = refs[4 * count], refs[4 * count + 1 :]
    acc_ref = None
    if start_from:
        acc_ref, refs = refs[0], refs[1:]
    out_ref, a_all, b_all, left_sems, right_sems = refs
    tiles = Tiles(where, items)
    wait_right = start_right(tiles, right, b_all, right_sems)
    wait_left = start_left(tiles, left, a_all, left_sems, 0, 1024)
    for item in range(len(items)):
        wait_right(item)
        wait_left(item)
    multiply(tiles, fock_ref, acc_ref, out_ref, a_all, b_all, 0)


def last_kernel(items, count, where, *refs):
    left, right = paired(refs[: 2 * count]), paired(refs[2 * count : 4 * count])
    fock_ref, acc_ref, out_ref, a_all, b_all, left_sems, right_sems = refs[4 * count :]
    tiles = Tiles(where, items)
    wait_right = start_right(tiles, right, b_all, right_sems)
    row_start = pl.multiple_of((1 - where[2]) * 512, 512)
    wait_left = start_left(tiles, left, a_all, left_sems.at[0], row_start, 512)
    kept = pl.multiple_of(where[2] * 512, 512)
    wait_kept = start_left(tiles, left, a_all, left_sems.at[1], kept, 512)
    for item in range(len(items)):
        wait_right(item)
        wait_left(item)
    multiply(tiles, fock_ref, acc_ref, out_ref, a_all, b_all, row_start)
    for item in range(len(items)):
        wait_kept(item)


def rest_kernel(items, where, a_all, b_all, fock_ref, acc_ref, out_ref):
    tiles = Tiles(where, items)
    row_start = pl.multiple_of(where[2] * 512, 512)
    multiply(tiles, fock_ref, acc_ref, out_ref, a_all, b_all, row_start)


ANYWHERE = pl.BlockSpec(memory_space=pl.ANY)
HBM = pl.BlockSpec(memory_space=pltpu.HBM)
VMEM = pl.BlockSpec(memory_space=pltpu.VMEM)
SMEM = pl.BlockSpec(memory_space=pltpu.SMEM)
LIMIT = pltpu.CompilerParams(vmem_limit_bytes=16 * 2**20)
FIRST = ((0, 0), (0, 1), (1, 0), (1, 1))
SECOND = ((0, 2), (2, 0), (1, 2), (2, 1), (2, 2))
THIRD = ((0, 3), (3, 0), (1, 3), (3, 1), (2, 3), (3, 2), (3, 3))


def cost(rows, items):
    return pl.CostEstimate(
        flops=2 * rows * 1280 * 256 * len(items),
        bytes_accessed=len(items) * 2**20,
        transcendentals=0,
    )


def flat(blocks, stay=8):
    halves = [half for block in blocks for half in block]
    return [
        pltpu.with_memory_space_constraint(half, pltpu.HBM) if n < 2 * stay else half
        for n, half in enumerate(halves)
    ]


def add_part(acc, where, left, right, fock_columns, items):
    start_from = acc is not None
    count = len(left)
    return pl.pallas_call(
        functools.partial(part_kernel, start_from, items, count),
        in_specs=[SMEM] + [HBM] * 4 * count + [VMEM] * (1 + start_from),
        out_specs=VMEM,
        scratch_shapes=[
            pltpu.VMEM((1024, 256 * len(items)), jnp.bfloat16),
            pltpu.VMEM((256 * len(items), 1024), jnp.bfloat16),
            pltpu.SemaphoreType.DMA((len(items), 2)),
            pltpu.SemaphoreType.DMA((len(items), 2)),
        ],
        out_shape=jax.ShapeDtypeStruct((1024, 1024), jnp.float32),
        input_output_aliases={4 * count + 2: 0} if start_from else {},
        compiler_params=LIMIT,
        cost_estimate=cost(1024, items),
        name="add_part",
    )(where, *flat(left), *flat(right), fock_columns, *([acc] * start_from))


def last_part(acc, where, left, right, fock_columns, items):
    count = len(left)
    return pl.pallas_call(
        functools.partial(last_kernel, items, count),
        in_specs=[SMEM] + [HBM] * 4 * count + [VMEM] * 2,
        out_specs=[VMEM] * 3,
        scratch_shapes=[
            pltpu.SemaphoreType.DMA((2, len(items), 2)),
            pltpu.SemaphoreType.DMA((len(items), 2)),
        ],
        out_shape=[
            jax.ShapeDtypeStruct((512, 1024), jnp.float32),
            jax.ShapeDtypeStruct((1024, 256 * len(items)), jnp.bfloat16),
            jax.ShapeDtypeStruct((256 * len(items), 1024), jnp.bfloat16),
        ],
        compiler_params=LIMIT,
        cost_estimate=cost(512, items),
        name="last_part",
    )(where, *flat(left, STAY), *flat(right, STAY), fock_columns, acc)


def rest_of_part(acc, where, a_all, b_all, fock_columns, items):
    return pl.pallas_call(
        functools.partial(rest_kernel, items),
        in_specs=[SMEM] + [VMEM] * 4,
        out_specs=VMEM,
        out_shape=jax.ShapeDtypeStruct((512, 1024), jnp.float32),
        compiler_params=LIMIT,
        cost_estimate=cost(512, items),
        name="rest_of_part",
    )(where, a_all, b_all, fock_columns, acc)


def update_kernel(where, flags_ref, occ_ref, virt_ref, own_ref, other_ref, amps_ref, out_ref, amps, new, sems):
    p, v, core = where[0], where[1], where[2]
    row_start = pl.multiple_of(core * 512, 512)
    load = pltpu.make_async_copy(amps_ref.at[0, :, pl.ds(row_start, 512), :], amps, sems.at[8])
    load.start()
    across = jnp.transpose(virt_ref[...])
    rows = [jnp.where(core == 0, across[:, t : t + 1], across[:, t + 4 : t + 5]) for t in range(4)]
    base = virt_ref[pl.ds(v, 1), :] - occ_ref[p]
    sums = [jnp.broadcast_to(row, (TILE, TILE)) + base for row in rows]
    load.wait()
    stores = []
    for j in range(8):
        for t in range(4):
            part = slice(t * TILE, (t + 1) * TILE)
            columns = slice(j * TILE, (j + 1) * TILE)
            keep = flags_ref[j, 4 * core + t].astype(jnp.float32)
            masked = amps[j, part, :].astype(jnp.float32) * keep
            residual = keep * (own_ref[part, columns] + other_ref[part, columns])
            new[j, part, :] = masked + residual / (sums[t] - occ_ref[j])
        store = pltpu.make_async_copy(new.at[j], out_ref.at[0, j], sems.at[j])
        store.start()
        stores.append(store)
    for store in stores:
        store.wait()


def update(where, flags, occ_energy, virt_energy, own_part, arrived, amplitudes):
    return pl.pallas_call(
        update_kernel,
        in_specs=[SMEM, SMEM, SMEM, VMEM, VMEM, VMEM, ANYWHERE],
        out_specs=ANYWHERE,
        out_shape=jax.ShapeDtypeStruct((1, 8, 512, TILE), jnp.float32),
        scratch_shapes=[
            pltpu.VMEM((8, 512, TILE), jnp.bfloat16),
            pltpu.VMEM((8, 512, TILE), jnp.float32),
            pltpu.SemaphoreType.DMA((9,)),
        ],
        compiler_params=LIMIT,
        name="update",
    )(where, flags, occ_energy, virt_energy, own_part, arrived, amplitudes)


def local(amplitudes, tile_mask, hole_integrals, virt_fock, occ_energy, virt_energy):
    p, v, r = (lax.axis_index(name) for name in AXES)
    flags = lax.dynamic_slice(tile_mask, (p, 0, 0, v), (1, 8, 8, 1)).reshape(8, 8)

    def half_of(block, half, pick):
        sizes = (1, 2, 1) + block.shape[3:]
        starts = (half, 0, pick) + (0,) * (block.ndim - 3)
        return lax.dynamic_slice(block, starts, sizes).reshape((2,) + block.shape[3:])

    def left_half(half):
        pick = (r + bit_of(v) + half) % 2
        kept = half_of(flags.reshape(2, 2, 2, 8), half, pick).astype(jnp.bfloat16)
        amps = half_of(amplitudes.reshape(2, 2, 2, 1024, TILE), half, pick)
        return amps * jnp.broadcast_to(kept[:, :, None], (2, 8, TILE)).reshape(2, 1024, 1)

    def right_half(half):
        pick = (r + bit_of(p) + half) % 2
        return half_of(hole_integrals.reshape(2, 2, 2, TILE, 8, TILE), half, pick).reshape(256, 1024)

    left = [[left_half(0), left_half(1)]]
    right = [[right_half(0), right_half(1)]]
    where = jnp.stack([p, v, r]).astype(jnp.int32)
    fock_columns = virt_fock.T
    for step in range(1, 8):
        passing = left[-1]
        if step == GATE:
            acc = add_part(None, where, left[:4], right[:4], fock_columns, FIRST)
            passing = [gate([passing[0]], [acc])[0], passing[1]]
            left[-1] = passing
        left.append([send(half, ALONG_VIRT) for half in passing])
        right.append([send(half, ALONG_PAIR) for half in right[-1]])
    acc = add_part(acc, where, left[:6], right[:6], fock_columns, SECOND)
    other_part, a_all, b_all = last_part(acc, where, left, right, fock_columns, THIRD)
    arrived = send(other_part, CORES)
    own_part = rest_of_part(acc, where, a_all, b_all, fock_columns, THIRD)
    return update(where, flags, occ_energy, virt_energy.reshape(8, TILE), own_part, arrived, amplitudes)


def solution(mesh):
    return jax.shard_map(
        local,
        mesh=mesh,
        in_specs=(
            P("pair", None, None, "virt"),
            P(),
            P("pair", None, None, "virt"),
            P("virt", None),
            P(),
            P(),
        ),
        out_specs=P("pair", None, "rep", "virt"),
        check_vma=False,
    )
```

```python
import functools

import jax
import jax.numpy as jnp
from jax import lax
from jax.experimental import pallas as pl
from jax.experimental.pallas import tpu as pltpu
from jax.sharding import PartitionSpec as P

TILE = 128
LIM = 20
EG = ((0, 3), (3, 9))
LG = ((0, 2), (2, 7))
WIDTH, STAY = 1024, 6
AXES = ("pair", "virt", "rep")


def device_permutation(move):
    pairs = []
    for index in range(128):
        p, v, core = index // 16, (index // 2) % 8, index % 2
        y, x, z, core = move((p // 4) * 2 + v // 4, p % 4, v % 4, core)
        pairs.append((index, ((y // 2) * 4 + x % 4) * 16 + ((y % 2) * 4 + z % 4) * 2 + core))
    return pairs


def ring_next(plane, place, cross):
    if plane == 0:
        return (1, place) if place == cross else (0, (place + 1) % 4)
    return (0, place) if place == (cross + 1) % 4 else (1, (place + 3) % 4)


def ring_move(plane, place, cross, core):
    if core == 0:
        return ring_next(plane, place, cross)
    return next(
        (a, b) for a in range(2) for b in range(4) if ring_next(a, b, cross) == (plane, place)
    )


def along_virt(y, x, z, core):
    low, z = ring_move(y % 2, z, 0 if x < 2 else 2, core)
    return (y // 2) * 2 + low, x, z, core


def along_pair(y, x, z, core):
    high, x = ring_move(y // 2, x, 2 if z < 2 else 0, core)
    return high * 2 + y % 2, x, z, core


ALONG_VIRT = device_permutation(along_virt)
ALONG_PAIR = device_permutation(along_pair)
CORES = device_permutation(lambda y, x, z, c: (y, x, z, 1 - c))


def send(block, permutation):
    return lax.ppermute(block, AXES, permutation)


def bit_of(index):
    return (index + index // 4) % 2


def on_ring(index, cross, core, step):
    plane, place = index // 4, index % 4
    spot = jnp.where(plane == 0, (place - cross + 3) % 4, 4 + (cross - place + 4) % 4)
    spot = (spot + 8 - (1 - 2 * core) * step) % 8
    return jnp.where(spot < 4, (spot + cross + 1) % 4, 4 + (cross - spot + 8) % 4)


class Tiles:
    def __init__(self, where, items):
        p, v, core = where[0], where[1], where[2]
        self.items = items
        self.odd = (core + bit_of(p) + bit_of(v)) % 2
        cross = jnp.where(p % 4 < 2, 0, 2)
        self.v = [on_ring(v, cross, core, q) for q in range(8)]
        cross = jnp.where(v % 4 < 2, 2, 0)
        self.k = [on_ring(p, cross, core, q) for q in range(8)]

    def pairs(self, item):
        i, j = self.items[item]
        for t in range(2):
            second = (self.odd + t) % 2
            k = jnp.where(second == 0, self.k[2 * j], self.k[2 * j + 1])
            yield t, 2 * i + t, self.v[2 * i + t], second, k


def start_left(tiles, left, a_all, sems, row_start, rows, some):
    part = pl.ds(row_start, rows)
    for item in some:
        for t, q, _, _, k in tiles.pairs(item):
            for half in range(2):

                @pl.when(k // 4 == half)
                def _():
                    pltpu.make_async_copy(
                        left[q][half].at[(k % 4) // 2, part, :],
                        a_all.at[part, (2 * item + t) * TILE : (2 * item + t + 1) * TILE],
                        sems.at[item, t],
                    ).start()

    def wait(item):
        i = tiles.items[item][0]
        for t in range(2):
            pltpu.make_async_copy(
                left[2 * i + t][0].at[0, part, :],
                a_all.at[part, (2 * item + t) * TILE : (2 * item + t + 1) * TILE],
                sems.at[item, t],
            ).wait()

    return wait


def start_right(tiles, right, b_all, sems, some):
    for item in some:
        j = tiles.items[item][1]
        for t, _, v, second, _ in tiles.pairs(item):
            for which in range(2):
                for half in range(2):

                    @pl.when((second == which) & (v // 4 == half))
                    def _():
                        rows = pl.ds(pl.multiple_of(((v % 4) // 2) * TILE, TILE), TILE)
                        pltpu.make_async_copy(
                            right[2 * j + which][half].at[rows, :],
                            b_all.at[(2 * item + t) * TILE : (2 * item + t + 1) * TILE, :],
                            sems.at[item, t],
                        ).start()

    def wait(item):
        j = tiles.items[item][1]
        for t in range(2):
            pltpu.make_async_copy(
                right[2 * j][0].at[pl.ds(0, TILE), :],
                b_all.at[(2 * item + t) * TILE : (2 * item + t + 1) * TILE, :],
                sems.at[item, t],
            ).wait()

    return wait


def multiply(tiles, some, fock_ref, acc_ref, out_ref, a_all, b_all, row_start):
    rows, width, block = out_ref.shape[0], WIDTH, 512
    depth = slice(some[0] * 256, (some[-1] + 1) * 256)

    def columns_of(step, carry):
        columns = pl.ds(pl.multiple_of(step * width, width), width)
        for row in range(0, rows, block):
            source = pl.ds(row_start + row, block)
            total = jnp.dot(
                a_all[source, depth], b_all[depth, columns], preferred_element_type=jnp.float32
            )
            if acc_ref is out_ref:
                total += out_ref[pl.ds(row, block), columns]
            elif acc_ref is not None:
                total += acc_ref[source, columns]
            out_ref[pl.ds(row, block), columns] = total
        return carry

    lax.fori_loop(0, 1024 // width, columns_of, 0)
    blank = jnp.zeros((TILE, TILE), jnp.bfloat16)
    for item in some:
        fock, places = [], []
        for t, _, v, _, k in tiles.pairs(item):
            own = fock_ref[pl.ds(pl.multiple_of(v * TILE, TILE), TILE), :]
            fock.append(jnp.concatenate([own, blank] if t == 0 else [blank, own], axis=1))
            places.append(pl.ds(pl.multiple_of(k * TILE, TILE), TILE))
        fock = jnp.concatenate(fock, axis=0)
        for row in range(0, rows, block):
            part = pl.ds(row, block)
            left = a_all[pl.ds(row_start + row, block), item * 256 : (item + 1) * 256]
            total = jnp.dot(left, fock, preferred_element_type=jnp.float32)
            for t in range(2):
                out_ref[part, places[t]] += total[:, t * TILE : (t + 1) * TILE]


def paired(refs):
    return [refs[n : n + 2] for n in range(0, len(refs), 2)]


def early_kernel(items, count, where, *refs):
    left, right = paired(refs[: 2 * count]), paired(refs[2 * count : 4 * count])
    fock_ref, out_ref, a_all, b_all, left_sems, right_sems = refs[4 * count :]
    tiles = Tiles(where, items)
    waits = []
    for some in EARLY_GROUPS:
        wait_right = start_right(tiles, right, b_all, right_sems, some)
        wait_left = start_left(tiles, left, a_all, left_sems, 0, 1024, some)
        waits.append((wait_right, wait_left))
    for some, (wait_right, wait_left) in zip(EARLY_GROUPS, waits):
        for item in some:
            wait_right(item)
            wait_left(item)
        source = out_ref if some[0] else None
        multiply(tiles, some, fock_ref, source, out_ref, a_all, b_all, 0)


def last_kernel(items, count, where, *refs):
    left, right = paired(refs[: 2 * count]), paired(refs[2 * count : 4 * count])
    fock_ref, acc_ref, out_ref, a_all, b_all, left_sems, right_sems = refs[4 * count :]
    tiles = Tiles(where, items)
    row_start = pl.multiple_of((1 - where[2]) * 512, 512)
    waits = []
    for some in LAST_GROUPS:
        wait_right = start_right(tiles, right, b_all, right_sems, some)
        wait_left = start_left(tiles, left, a_all, left_sems, 0, 1024, some)
        waits.append((wait_right, wait_left))
    for some, (wait_right, wait_left) in zip(LAST_GROUPS, waits):
        for item in some:
            wait_right(item)
            wait_left(item)
        source = out_ref if some[0] else acc_ref
        multiply(tiles, some, fock_ref, source, out_ref, a_all, b_all, row_start)


def rest_kernel(items, where, a_all, b_all, fock_ref, acc_ref, out_ref):
    tiles = Tiles(where, items)
    row_start = pl.multiple_of(where[2] * 512, 512)
    multiply(tiles, range(len(items)), fock_ref, acc_ref, out_ref, a_all, b_all, row_start)


ANYWHERE = pl.BlockSpec(memory_space=pl.ANY)
HBM = pl.BlockSpec(memory_space=pltpu.HBM)
VMEM = pl.BlockSpec(memory_space=pltpu.VMEM)
SMEM = pl.BlockSpec(memory_space=pltpu.SMEM)
LIMIT = pltpu.CompilerParams(vmem_limit_bytes=LIM * 2**20)
FIRST = ((0, 0), (0, 1), (1, 0), (1, 1))
SECOND = ((0, 2), (2, 0), (1, 2), (2, 1), (2, 2))
THIRD = ((0, 3), (3, 0), (1, 3), (3, 1), (2, 3), (3, 2), (3, 3))

EARLY_GROUPS = tuple(range(n, m) for n, m in EG)
LAST_GROUPS = tuple(range(n, m) for n, m in LG)


def cost(rows, items):
    return pl.CostEstimate(
        flops=2 * rows * 1280 * 256 * len(items),
        bytes_accessed=len(items) * 2**20,
        transcendentals=0,
    )


def flat(blocks, stay=8):
    halves = [half for block in blocks for half in block]
    return [
        pltpu.with_memory_space_constraint(half, pltpu.HBM) if n < 2 * stay else half
        for n, half in enumerate(halves)
    ]


def early_part(where, left, right, fock_columns, items):
    count = len(left)
    return pl.pallas_call(
        functools.partial(early_kernel, items, count),
        in_specs=[SMEM] + [HBM] * 4 * count + [VMEM],
        out_specs=VMEM,
        scratch_shapes=[
            pltpu.VMEM((1024, 256 * len(items)), jnp.bfloat16),
            pltpu.VMEM((256 * len(items), 1024), jnp.bfloat16),
            pltpu.SemaphoreType.DMA((len(items), 2)),
            pltpu.SemaphoreType.DMA((len(items), 2)),
        ],
        out_shape=jax.ShapeDtypeStruct((1024, 1024), jnp.float32),
        compiler_params=LIMIT,
        cost_estimate=cost(1024, items),
        name="early_part",
    )(where, *flat(left), *flat(right), fock_columns)


def last_part(acc, where, left, right, fock_columns, items):
    count = len(left)
    return pl.pallas_call(
        functools.partial(last_kernel, items, count),
        in_specs=[SMEM] + [HBM] * 4 * count + [VMEM] * 2,
        out_specs=[VMEM] * 3,
        scratch_shapes=[
            pltpu.SemaphoreType.DMA((len(items), 2)),
            pltpu.SemaphoreType.DMA((len(items), 2)),
        ],
        out_shape=[
            jax.ShapeDtypeStruct((512, 1024), jnp.float32),
            jax.ShapeDtypeStruct((1024, 256 * len(items)), jnp.bfloat16),
            jax.ShapeDtypeStruct((256 * len(items), 1024), jnp.bfloat16),
        ],
        compiler_params=LIMIT,
        cost_estimate=cost(512, items),
        name="last_part",
    )(where, *flat(left, STAY), *flat(right, STAY), fock_columns, acc)


def rest_of_part(acc, where, a_all, b_all, fock_columns, items):
    return pl.pallas_call(
        functools.partial(rest_kernel, items),
        in_specs=[SMEM] + [VMEM] * 4,
        out_specs=VMEM,
        out_shape=jax.ShapeDtypeStruct((512, 1024), jnp.float32),
        compiler_params=LIMIT,
        cost_estimate=cost(512, items),
        name="rest_of_part",
    )(where, a_all, b_all, fock_columns, acc)


def update_kernel(where, flags_ref, occ_ref, virt_ref, own_ref, other_ref, amps_ref, out_ref, amps, new, sems):
    p, v, core = where[0], where[1], where[2]
    row_start = pl.multiple_of(core * 512, 512)
    load = pltpu.make_async_copy(amps_ref.at[0, :, pl.ds(row_start, 512), :], amps, sems.at[8])
    load.start()
    across = jnp.transpose(virt_ref[...])
    rows = [jnp.where(core == 0, across[:, t : t + 1], across[:, t + 4 : t + 5]) for t in range(4)]
    base = virt_ref[pl.ds(v, 1), :] - occ_ref[p]
    sums = [jnp.broadcast_to(row, (TILE, TILE)) + base for row in rows]
    load.wait()
    stores = []
    for j in range(8):
        for t in range(4):
            part = slice(t * TILE, (t + 1) * TILE)
            columns = slice(j * TILE, (j + 1) * TILE)
            keep = flags_ref[j, 4 * core + t].astype(jnp.float32)
            masked = amps[j, part, :].astype(jnp.float32) * keep
            residual = keep * (own_ref[part, columns] + other_ref[part, columns])
            new[j, part, :] = masked + residual / (sums[t] - occ_ref[j])
        store = pltpu.make_async_copy(new.at[j], out_ref.at[0, j], sems.at[j])
        store.start()
        stores.append(store)
    for store in stores:
        store.wait()


def update(where, flags, occ_energy, virt_energy, own_part, arrived, amplitudes):
    return pl.pallas_call(
        update_kernel,
        in_specs=[SMEM, SMEM, SMEM, VMEM, VMEM, VMEM, ANYWHERE],
        out_specs=ANYWHERE,
        out_shape=jax.ShapeDtypeStruct((1, 8, 512, TILE), jnp.float32),
        scratch_shapes=[
            pltpu.VMEM((8, 512, TILE), jnp.bfloat16),
            pltpu.VMEM((8, 512, TILE), jnp.float32),
            pltpu.SemaphoreType.DMA((9,)),
        ],
        compiler_params=LIMIT,
        name="update",
    )(where, flags, occ_energy, virt_energy, own_part, arrived, amplitudes)


def local(amplitudes, tile_mask, hole_integrals, virt_fock, occ_energy, virt_energy):
    p, v, r = (lax.axis_index(name) for name in AXES)
    flags = lax.dynamic_slice(tile_mask, (p, 0, 0, v), (1, 8, 8, 1)).reshape(8, 8)

    def half_of(block, half, pick):
        sizes = (1, 2, 1) + block.shape[3:]
        starts = (half, 0, pick) + (0,) * (block.ndim - 3)
        return lax.dynamic_slice(block, starts, sizes).reshape((2,) + block.shape[3:])

    def left_half(half):
        pick = (r + bit_of(v) + half) % 2
        kept = half_of(flags.reshape(2, 2, 2, 8), half, pick).astype(jnp.bfloat16)
        amps = half_of(amplitudes.reshape(2, 2, 2, 1024, TILE), half, pick)
        return amps * jnp.broadcast_to(kept[:, :, None], (2, 8, TILE)).reshape(2, 1024, 1)

    def right_half(half):
        pick = (r + bit_of(p) + half) % 2
        return half_of(hole_integrals.reshape(2, 2, 2, TILE, 8, TILE), half, pick).reshape(256, 1024)

    left = [[left_half(0), left_half(1)]]
    right = [[right_half(0), right_half(1)]]
    where = jnp.stack([p, v, r]).astype(jnp.int32)
    fock_columns = virt_fock.T
    for _ in range(7):
        left.append([send(half, ALONG_VIRT) for half in left[-1]])
        right.append([send(half, ALONG_PAIR) for half in right[-1]])
    acc = early_part(where, left[:6], right[:6], fock_columns, FIRST + SECOND)
    other_part, a_all, b_all = last_part(acc, where, left, right, fock_columns, THIRD)
    arrived = send(other_part, CORES)
    own_part = rest_of_part(acc, where, a_all, b_all, fock_columns, THIRD)
    return update(where, flags, occ_energy, virt_energy.reshape(8, TILE), own_part, arrived, amplitudes)


def solution(mesh):
    return jax.shard_map(
        local,
        mesh=mesh,
        in_specs=(
            P("pair", None, None, "virt"),
            P(),
            P("pair", None, None, "virt"),
            P("virt", None),
            P(),
            P(),
        ),
        out_specs=P("pair", None, "rep", "virt"),
        check_vma=False,
    )
```

```python
import functools

import jax
import jax.numpy as jnp
from jax import lax
from jax.experimental import pallas as pl
from jax.experimental.pallas import tpu as pltpu
from jax.sharding import PartitionSpec as P

TILE = 128
LIM = 20
EG = ((0, 3), (3, 9))
LG = ((0, 2), (2, 7))
WIDTH, STAY = 1024, 6
AXES = ("pair", "virt", "rep")


def device_permutation(move):
    pairs = []
    for index in range(128):
        p, v, core = index // 16, (index // 2) % 8, index % 2
        y, x, z, core = move((p // 4) * 2 + v // 4, p % 4, v % 4, core)
        pairs.append((index, ((y // 2) * 4 + x % 4) * 16 + ((y % 2) * 4 + z % 4) * 2 + core))
    return pairs


def ring_next(plane, place, cross):
    if plane == 0:
        return (1, place) if place == cross else (0, (place + 1) % 4)
    return (0, place) if place == (cross + 1) % 4 else (1, (place + 3) % 4)


def ring_move(plane, place, cross, core):
    if core == 0:
        return ring_next(plane, place, cross)
    return next(
        (a, b) for a in range(2) for b in range(4) if ring_next(a, b, cross) == (plane, place)
    )


def along_virt(y, x, z, core):
    low, z = ring_move(y % 2, z, 0 if x < 2 else 2, core)
    return (y // 2) * 2 + low, x, z, core


def along_pair(y, x, z, core):
    high, x = ring_move(y // 2, x, 2 if z < 2 else 0, core)
    return high * 2 + y % 2, x, z, core


ALONG_VIRT = device_permutation(along_virt)
ALONG_PAIR = device_permutation(along_pair)
CORES = device_permutation(lambda y, x, z, c: (y, x, z, 1 - c))


def send(block, permutation):
    return lax.ppermute(block, AXES, permutation)


def bit_of(index):
    return (index + index // 4) % 2


def on_ring(index, cross, core, step):
    plane, place = index // 4, index % 4
    spot = jnp.where(plane == 0, (place - cross + 3) % 4, 4 + (cross - place + 4) % 4)
    spot = (spot + 8 - (1 - 2 * core) * step) % 8
    return jnp.where(spot < 4, (spot + cross + 1) % 4, 4 + (cross - spot + 8) % 4)


class Tiles:
    def __init__(self, where, items):
        p, v, core = where[0], where[1], where[2]
        self.items = items
        self.odd = (core + bit_of(p) + bit_of(v)) % 2
        cross = jnp.where(p % 4 < 2, 0, 2)
        self.v = [on_ring(v, cross, core, q) for q in range(8)]
        cross = jnp.where(v % 4 < 2, 2, 0)
        self.k = [on_ring(p, cross, core, q) for q in range(8)]

    def pairs(self, item):
        i, j = self.items[item]
        for t in range(2):
            second = (self.odd + t) % 2
            k = jnp.where(second == 0, self.k[2 * j], self.k[2 * j + 1])
            yield t, 2 * i + t, self.v[2 * i + t], second, k


def start_left(tiles, left, a_all, sems, row_start, rows, some):
    part = pl.ds(row_start, rows)
    for item in some:
        for t, q, _, _, k in tiles.pairs(item):
            for half in range(2):

                @pl.when(k // 4 == half)
                def _():
                    pltpu.make_async_copy(
                        left[q][half].at[(k % 4) // 2, part, :],
                        a_all.at[part, (2 * item + t) * TILE : (2 * item + t + 1) * TILE],
                        sems.at[item, t],
                    ).start()

    def wait(item):
        i = tiles.items[item][0]
        for t in range(2):
            pltpu.make_async_copy(
                left[2 * i + t][0].at[0, part, :],
                a_all.at[part, (2 * item + t) * TILE : (2 * item + t + 1) * TILE],
                sems.at[item, t],
            ).wait()

    return wait


def start_right(tiles, right, b_all, sems, some):
    for item in some:
        j = tiles.items[item][1]
        for t, _, v, second, _ in tiles.pairs(item):
            for which in range(2):
                for half in range(2):

                    @pl.when((second == which) & (v // 4 == half))
                    def _():
                        rows = pl.ds(pl.multiple_of(((v % 4) // 2) * TILE, TILE), TILE)
                        pltpu.make_async_copy(
                            right[2 * j + which][half].at[rows, :],
                            b_all.at[(2 * item + t) * TILE : (2 * item + t + 1) * TILE, :],
                            sems.at[item, t],
                        ).start()

    def wait(item):
        j = tiles.items[item][1]
        for t in range(2):
            pltpu.make_async_copy(
                right[2 * j][0].at[pl.ds(0, TILE), :],
                b_all.at[(2 * item + t) * TILE : (2 * item + t + 1) * TILE, :],
                sems.at[item, t],
            ).wait()

    return wait


def multiply(tiles, some, fock_ref, acc_ref, out_ref, a_all, b_all, row_start):
    rows, width, block = out_ref.shape[0], WIDTH, 256
    depth = slice(some[0] * 256, (some[-1] + 1) * 256)

    def columns_of(step, carry):
        columns = pl.ds(pl.multiple_of(step * width, width), width)
        for row in range(0, rows, block):
            source = pl.ds(row_start + row, block)
            total = jnp.dot(
                a_all[source, depth], b_all[depth, columns], preferred_element_type=jnp.float32
            )
            if acc_ref is out_ref:
                total += out_ref[pl.ds(row, block), columns]
            elif acc_ref is not None:
                total += acc_ref[source, columns]
            out_ref[pl.ds(row, block), columns] = total
        return carry

    lax.fori_loop(0, 1024 // width, columns_of, 0)
    blank = jnp.zeros((TILE, TILE), jnp.bfloat16)
    for item in some:
        fock, places = [], []
        for t, _, v, _, k in tiles.pairs(item):
            own = fock_ref[pl.ds(pl.multiple_of(v * TILE, TILE), TILE), :]
            fock.append(jnp.concatenate([own, blank] if t == 0 else [blank, own], axis=1))
            places.append(pl.ds(pl.multiple_of(k * TILE, TILE), TILE))
        fock = jnp.concatenate(fock, axis=0)
        for row in range(0, rows, block):
            part = pl.ds(row, block)
            left = a_all[pl.ds(row_start + row, block), item * 256 : (item + 1) * 256]
            total = jnp.dot(left, fock, preferred_element_type=jnp.float32)
            for t in range(2):
                out_ref[part, places[t]] += total[:, t * TILE : (t + 1) * TILE]


def paired(refs):
    return [refs[n : n + 2] for n in range(0, len(refs), 2)]


def early_kernel(items, count, where, *refs):
    left, right = paired(refs[: 2 * count]), paired(refs[2 * count : 4 * count])
    fock_ref, out_ref, a_all, b_all, left_sems, right_sems = refs[4 * count :]
    tiles = Tiles(where, items)
    waits = []
    for some in EARLY_GROUPS:
        wait_right = start_right(tiles, right, b_all, right_sems, some)
        wait_left = start_left(tiles, left, a_all, left_sems, 0, 1024, some)
        waits.append((wait_right, wait_left))
    for some, (wait_right, wait_left) in zip(EARLY_GROUPS, waits):
        for item in some:
            wait_right(item)
            wait_left(item)
        source = out_ref if some[0] else None
        multiply(tiles, some, fock_ref, source, out_ref, a_all, b_all, 0)


def last_kernel(items, count, where, *refs):
    left, right = paired(refs[: 2 * count]), paired(refs[2 * count : 4 * count])
    fock_ref, acc_ref, out_ref, a_all, b_all, left_sems, right_sems = refs[4 * count :]
    tiles = Tiles(where, items)
    row_start = pl.multiple_of((1 - where[2]) * 512, 512)
    waits = []
    for some in LAST_GROUPS:
        wait_right = start_right(tiles, right, b_all, right_sems, some)
        wait_left = start_left(tiles, left, a_all, left_sems, 0, 1024, some)
        waits.append((wait_right, wait_left))
    for some, (wait_right, wait_left) in zip(LAST_GROUPS, waits):
        for item in some:
            wait_right(item)
            wait_left(item)
        source = out_ref if some[0] else acc_ref
        multiply(tiles, some, fock_ref, source, out_ref, a_all, b_all, row_start)


def rest_kernel(items, where, a_all, b_all, fock_ref, acc_ref, out_ref):
    tiles = Tiles(where, items)
    row_start = pl.multiple_of(where[2] * 512, 512)
    multiply(tiles, range(len(items)), fock_ref, acc_ref, out_ref, a_all, b_all, row_start)


ANYWHERE = pl.BlockSpec(memory_space=pl.ANY)
HBM = pl.BlockSpec(memory_space=pltpu.HBM)
VMEM = pl.BlockSpec(memory_space=pltpu.VMEM)
SMEM = pl.BlockSpec(memory_space=pltpu.SMEM)
LIMIT = pltpu.CompilerParams(vmem_limit_bytes=LIM * 2**20)
FIRST = ((0, 0), (0, 1), (1, 0), (1, 1))
SECOND = ((0, 2), (2, 0), (1, 2), (2, 1), (2, 2))
THIRD = ((0, 3), (3, 0), (1, 3), (3, 1), (2, 3), (3, 2), (3, 3))

EARLY_GROUPS = tuple(range(n, m) for n, m in EG)
LAST_GROUPS = tuple(range(n, m) for n, m in LG)


def cost(rows, items):
    return pl.CostEstimate(
        flops=2 * rows * 1280 * 256 * len(items),
        bytes_accessed=len(items) * 2**20,
        transcendentals=0,
    )


def flat(blocks, stay=8):
    halves = [half for block in blocks for half in block]
    return [
        pltpu.with_memory_space_constraint(half, pltpu.HBM) if n < 2 * stay else half
        for n, half in enumerate(halves)
    ]


def early_part(where, left, right, fock_columns, items):
    count = len(left)
    return pl.pallas_call(
        functools.partial(early_kernel, items, count),
        in_specs=[SMEM] + [HBM] * 4 * count + [VMEM],
        out_specs=VMEM,
        scratch_shapes=[
            pltpu.VMEM((1024, 256 * len(items)), jnp.bfloat16),
            pltpu.VMEM((256 * len(items), 1024), jnp.bfloat16),
            pltpu.SemaphoreType.DMA((len(items), 2)),
            pltpu.SemaphoreType.DMA((len(items), 2)),
        ],
        out_shape=jax.ShapeDtypeStruct((1024, 1024), jnp.float32),
        compiler_params=LIMIT,
        cost_estimate=cost(1024, items),
        name="early_part",
    )(where, *flat(left), *flat(right), fock_columns)


def last_part(acc, where, left, right, fock_columns, items):
    count = len(left)
    return pl.pallas_call(
        functools.partial(last_kernel, items, count),
        in_specs=[SMEM] + [HBM] * 4 * count + [VMEM] * 2,
        out_specs=[VMEM] * 3,
        scratch_shapes=[
            pltpu.SemaphoreType.DMA((len(items), 2)),
            pltpu.SemaphoreType.DMA((len(items), 2)),
        ],
        out_shape=[
            jax.ShapeDtypeStruct((512, 1024), jnp.float32),
            jax.ShapeDtypeStruct((1024, 256 * len(items)), jnp.bfloat16),
            jax.ShapeDtypeStruct((256 * len(items), 1024), jnp.bfloat16),
        ],
        compiler_params=LIMIT,
        cost_estimate=cost(512, items),
        name="last_part",
    )(where, *flat(left, STAY), *flat(right, STAY), fock_columns, acc)


def rest_of_part(acc, where, a_all, b_all, fock_columns, items):
    return pl.pallas_call(
        functools.partial(rest_kernel, items),
        in_specs=[SMEM] + [VMEM] * 4,
        out_specs=VMEM,
        out_shape=jax.ShapeDtypeStruct((512, 1024), jnp.float32),
        compiler_params=LIMIT,
        cost_estimate=cost(512, items),
        name="rest_of_part",
    )(where, a_all, b_all, fock_columns, acc)


def update_kernel(where, flags_ref, occ_ref, virt_ref, own_ref, other_ref, amps_ref, out_ref, amps, new, sems):
    p, v, core = where[0], where[1], where[2]
    row_start = pl.multiple_of(core * 512, 512)
    load = pltpu.make_async_copy(amps_ref.at[0, :, pl.ds(row_start, 512), :], amps, sems.at[8])
    load.start()
    across = jnp.transpose(virt_ref[...])
    rows = [jnp.where(core == 0, across[:, t : t + 1], across[:, t + 4 : t + 5]) for t in range(4)]
    base = virt_ref[pl.ds(v, 1), :] - occ_ref[p]
    sums = [jnp.broadcast_to(row, (TILE, TILE)) + base for row in rows]
    load.wait()
    stores = []
    for j in range(8):
        for t in range(4):
            part = slice(t * TILE, (t + 1) * TILE)
            columns = slice(j * TILE, (j + 1) * TILE)
            keep = flags_ref[j, 4 * core + t].astype(jnp.float32)
            masked = amps[j, part, :].astype(jnp.float32) * keep
            residual = keep * (own_ref[part, columns] + other_ref[part, columns])
            new[j, part, :] = masked + residual / (sums[t] - occ_ref[j])
        store = pltpu.make_async_copy(new.at[j], out_ref.at[0, j], sems.at[j])
        store.start()
        stores.append(store)
    for store in stores:
        store.wait()


def update(where, flags, occ_energy, virt_energy, own_part, arrived, amplitudes):
    return pl.pallas_call(
        update_kernel,
        in_specs=[SMEM, SMEM, SMEM, VMEM, VMEM, VMEM, ANYWHERE],
        out_specs=ANYWHERE,
        out_shape=jax.ShapeDtypeStruct((1, 8, 512, TILE), jnp.float32),
        scratch_shapes=[
            pltpu.VMEM((8, 512, TILE), jnp.bfloat16),
            pltpu.VMEM((8, 512, TILE), jnp.float32),
            pltpu.SemaphoreType.DMA((9,)),
        ],
        compiler_params=LIMIT,
        name="update",
    )(where, flags, occ_energy, virt_energy, own_part, arrived, amplitudes)


def local(amplitudes, tile_mask, hole_integrals, virt_fock, occ_energy, virt_energy):
    p, v, r = (lax.axis_index(name) for name in AXES)
    flags = lax.dynamic_slice(tile_mask, (p, 0, 0, v), (1, 8, 8, 1)).reshape(8, 8)

    def half_of(block, half, pick):
        sizes = (1, 2, 1) + block.shape[3:]
        starts = (half, 0, pick) + (0,) * (block.ndim - 3)
        return lax.dynamic_slice(block, starts, sizes).reshape((2,) + block.shape[3:])

    def left_half(half):
        pick = (r + bit_of(v) + half) % 2
        kept = half_of(flags.reshape(2, 2, 2, 8), half, pick).astype(jnp.bfloat16)
        amps = half_of(amplitudes.reshape(2, 2, 2, 1024, TILE), half, pick)
        return amps * jnp.broadcast_to(kept[:, :, None], (2, 8, TILE)).reshape(2, 1024, 1)

    def right_half(half):
        pick = (r + bit_of(p) + half) % 2
        return half_of(hole_integrals.reshape(2, 2, 2, TILE, 8, TILE), half, pick).reshape(256, 1024)

    left = [[left_half(0), left_half(1)]]
    right = [[right_half(0), right_half(1)]]
    where = jnp.stack([p, v, r]).astype(jnp.int32)
    fock_columns = virt_fock.T
    for _ in range(7):
        left.append([send(half, ALONG_VIRT) for half in left[-1]])
        right.append([send(half, ALONG_PAIR) for half in right[-1]])
    acc = early_part(where, left[:6], right[:6], fock_columns, FIRST + SECOND)
    other_part, a_all, b_all = last_part(acc, where, left, right, fock_columns, THIRD)
    arrived = send(other_part, CORES)
    own_part = rest_of_part(acc, where, a_all, b_all, fock_columns, THIRD)
    return update(where, flags, occ_energy, virt_energy.reshape(8, TILE), own_part, arrived, amplitudes)


def solution(mesh):
    return jax.shard_map(
        local,
        mesh=mesh,
        in_specs=(
            P("pair", None, None, "virt"),
            P(),
            P("pair", None, None, "virt"),
            P("virt", None),
            P(),
            P(),
        ),
        out_specs=P("pair", None, "rep", "virt"),
        check_vma=False,
    )
```
